256 devices in a mesh: dp: 2 (over core), expert: 128 (over z, y, x).
Axes of the slice: x: 4, y: 4, z: 8, core: 2. Of those that a mesh axis runs over, the one named last changes fastest.
Arguments:
- inputs: bfloat16 [8192, 4096], P(('dp', 'expert')), may hold values from -6 to 6
- cotangent: bfloat16 [8192, 4096], P(('dp', 'expert')), may hold values from -6 to 6
- gates: bfloat16 [32768, 2], P(('dp', 'expert')), may hold values from 0.19921875 to 1
- routes: int32 [32768, 2], P(('dp', 'expert')), may hold values from 0 to 127, all different within a row; in each aligned block of 128 rows (0 to 127, 128 to 255, ...) at most 4 rows name the same one
- w_in: bfloat16 [128, 1024, 2048], P('expert', None, 'dp'), may hold values from -0.1875 to 0.1875
- w_out: bfloat16 [128, 2048, 1024], P('expert', 'dp'), may hold values from -0.125 to 0.125
Outputs:
- input_grad: bfloat16 [8192, 4096], P(('dp', 'expert'))
- gate_grad: float32 [32768, 2], P(('dp', 'expert'))
- w_in_grad: bfloat16 [128, 1024, 2048], P('expert', None, 'dp')
- w_out_grad: bfloat16 [128, 2048, 1024], P('expert', 'dp')
The draws below stay inside these ranges and needn't reach their ends.
Inputs may be any that keep to these rules, and one draw needn't show every extreme that they name: `routes`: within the sub-tokens of one device (aligned blocks of 128 rows), no expert is named more than 4 times, and in every block some expert is named exactly 4 times; the two experts of a row differ.
All inputs are finite; a program needn't handle non-finite values.
Results may differ from the reference program's by a relative error of at most 0.0058.
Values may be sent and summed in bfloat16 or wider, within the bound.
A program may use at most 128 MiB of HBM per device.

```python
import math
import jax
import jax.numpy as jnp
import numpy as np
from jax import lax

HEADS = 4
D_SUB = 1024
FF = 2048
TOK_DEV = 32
EXPERTS = 128
CAP = 4
TOKENS = 8192
SUBTOK = 32768
N_DP = 2
N_EXPERT = 128


def block_levels(key, dims, split, smallest, high):
    gain = 1.0
    for axis_at, blocks in split:
        heights = jax.random.uniform(jax.random.fold_in(jax.random.fold_in(key, 6), axis_at), (blocks,), jnp.float32, smallest / len(split), high / len(split))
        gain = gain * jnp.repeat(jnp.exp(heights), dims[axis_at] // blocks).reshape((-1,) + (1,) * (len(dims) - 1 - axis_at))
    return gain


def routed_block(key, own, number, rows, count, top, bound, slope):
    ranking = jax.random.permutation(key, count)
    packed, ordinary = portions_of(count, rows * top, bound, slope, True), portions_of(count, rows * top, bound, slope, False)
    places = jnp.arange(count)

    def named(lengths, rotation):
        used = int((lengths > 0).sum())
        fixed = max(1, used // 4)
        shifted = fixed + (places - fixed + rotation * (used - fixed)) % max(1, count - fixed)
        return jnp.zeros((count,), jnp.int32).at[ranking[jnp.where(places < fixed, places, shifted)]].set(jnp.asarray(lengths, jnp.int32))

    lengths = jnp.where(number % 4 == 0, named(packed, number // 4), named(ordinary, number - number // 4 - 1))
    mixed = jax.random.permutation(jax.random.fold_in(own, 3), count)
    source_of, receiver = mixed[0:count // 2 * 2:2], mixed[1:count // 2 * 2:2]
    margin = jnp.minimum(lengths[source_of] - 1, bound - lengths[receiver]) // 2
    margin = jnp.where((source_of == ranking[0]) | (receiver == ranking[0]) | (lengths[receiver] == 0), 0, jnp.maximum(margin, 0))
    shifted = jax.random.randint(jax.random.fold_in(own, 4), (count // 2,), 0, 1 << 20) % (margin + 1)
    lengths = lengths.at[source_of].add(-shifted).at[receiver].add(shifted)
    members = jnp.searchsorted(jnp.cumsum(lengths), jnp.arange(rows * top), side="right").astype(jnp.int32)
    listing = members.reshape(top, rows).T
    listing = listing[jax.random.permutation(jax.random.fold_in(own, 1), rows)]
    rotation = jax.random.randint(jax.random.fold_in(own, 2), (rows, 1), 0, top)
    return jnp.take_along_axis(listing, (jnp.arange(top)[None, :] + rotation) % top, axis=1)


def portions_of(amount, total, bound, skew, full):
    portions = [(1 << 20) // math.isqrt(grade ** skew) + 1 for grade in range(1, amount + 1)]
    largest = bound if full else min(bound, max(-(-total // amount), total * portions[0] // sum(portions)))
    least = 1 if total - largest >= amount - 1 else 0
    holding, spare = [largest] + [least] * (amount - 1), total - largest - least * (amount - 1)
    while spare > 0:
        movable = [i for i in range(1, amount) if holding[i] < largest] or [i for i in range(1, amount) if holding[i] < bound]
        pool, left = sum([portions[i] for i in movable]), spare
        for i in movable:
            more = min(bound - holding[i], max(1, left * portions[i] // pool), spare)
            holding[i] = holding[i] + more
            spare = spare - more
    return np.array(holding)


def centred(key, shape, spread, limit, pieces=(), kind=jnp.bfloat16):
    array = spread * jax.random.normal(key, shape, jnp.float32)
    if pieces:
        array = array * block_levels(key, shape, pieces, -0.22, 0.18)
    return jnp.clip(array, -limit, limit).astype(kind)


def setup_inputs(seed: int = 0) -> dict:
    keys = jax.random.split(jax.random.key(seed), 7)
    inputs = centred(keys[0], (TOKENS, HEADS * D_SUB), 1.0, 6.0, ((0, 256),))
    cotangent = centred(keys[1], (TOKENS, HEADS * D_SUB), 1.0, 6.0, ((0, 256),))
    gates = jnp.clip(0.19921875 + 0.80078125 * jax.random.uniform(keys[2], (SUBTOK, 2), jnp.float32) ** block_levels(keys[2], (SUBTOK, 2), ((0, 256),), -0.2, 0.2), 0.19921875, 1.0).astype(jnp.bfloat16)
    routes_keys = jax.random.split(jax.random.fold_in(keys[3], 1), SUBTOK // (TOK_DEV * HEADS))
    routes_turns = jax.random.permutation(jax.random.fold_in(keys[3], 3), SUBTOK // (TOK_DEV * HEADS))
    routes = jax.vmap(lambda own, number: routed_block(jax.random.fold_in(keys[3], 2), own, number, TOK_DEV * HEADS, EXPERTS, 2, CAP, 2))(routes_keys, routes_turns).reshape((SUBTOK, 2))
    w_in = centred(keys[4], (EXPERTS, D_SUB, FF), D_SUB ** -0.5, 0.1875, ((0, 128), (2, 2)))
    w_out = centred(keys[5], (EXPERTS, FF, D_SUB), FF ** -0.5, 0.125, ((0, 128), (1, 2)))
    return dict(inputs=inputs, cotangent=cotangent, gates=gates, routes=routes, w_in=w_in, w_out=w_out)


def gelu_tanh(values):
    inner = 0.7978845608028654 * (values + 0.044715 * values * values * values)
    return 0.5 * values * (1.0 + jnp.tanh(inner))


def gelu_slope(values):
    inner = 0.7978845608028654 * (values + 0.044715 * values * values * values)
    tangent = jnp.tanh(inner)
    return 0.5 * (1.0 + tangent) + 0.5 * values * (1.0 - tangent * tangent) * 0.7978845608028654 * (1.0 + 3.0 * 0.044715 * values * values)


def expert_terms(rows_in, rows_cot, rows_gate, weight_in, weight_out):
    hidden = jnp.dot(rows_in, weight_in, preferred_element_type=jnp.float32)
    active = gelu_tanh(hidden).astype(jnp.bfloat16)
    output = jnp.dot(active, weight_out, preferred_element_type=jnp.float32)
    dots = jnp.sum(output * rows_cot.astype(jnp.float32), axis=-1)
    scaled = (rows_gate.astype(jnp.float32)[:, None] * rows_cot.astype(jnp.float32)).astype(jnp.bfloat16)
    back_active = lax.dot_general(scaled, weight_out, (((1,), (1,)), ((), ())), preferred_element_type=jnp.float32)
    back_hidden = (back_active * gelu_slope(hidden)).astype(jnp.bfloat16)
    grad_out = lax.dot_general(active, scaled, (((0,), (0,)), ((), ())), preferred_element_type=jnp.float32)
    grad_in = lax.dot_general(rows_in, back_hidden, (((0,), (0,)), ((), ())), preferred_element_type=jnp.float32)
    row_grads = lax.dot_general(back_hidden, weight_in, (((1,), (1,)), ((), ())), preferred_element_type=jnp.float32)
    return grad_in, grad_out, row_grads, dots


def reference(inputs, cotangent, gates, routes, w_in, w_out):
    devices = N_DP * N_EXPERT
    local_rows = TOK_DEV * HEADS
    sub_inputs = inputs.reshape(devices * local_rows, D_SUB)
    sub_cot = cotangent.reshape(devices * local_rows, D_SUB)
    chosen = routes.reshape(devices, local_rows * 2)
    member = (chosen[:, :, None] == jnp.arange(EXPERTS, dtype=jnp.int32)[None, None, :]).astype(jnp.int32)
    earlier = jnp.cumsum(member, axis=1) - member
    slots = jnp.sum(earlier * member, axis=2).astype(jnp.int32)
    position = jnp.arange(devices, dtype=jnp.int32)[:, None] * CAP + slots
    buffer_rows = devices * CAP
    target = (chosen * buffer_rows + position).reshape(-1).astype(jnp.int32)
    source = (jnp.arange(devices * local_rows * 2, dtype=jnp.int32) // 2).astype(jnp.int32)
    total = EXPERTS * buffer_rows
    buf_in = jnp.zeros((total, D_SUB), jnp.bfloat16).at[target].set(sub_inputs[source])
    buf_cot = jnp.zeros((total, D_SUB), jnp.bfloat16).at[target].set(sub_cot[source])
    buf_gate = jnp.zeros((total,), jnp.bfloat16).at[target].set(gates.reshape(-1))

    def one_expert(items):
        rows_in, rows_cot, rows_gate, weight_in, weight_out = items
        grad_in, grad_out, row_grads, dots = expert_terms(rows_in, rows_cot, rows_gate, weight_in, weight_out)
        return grad_in.astype(jnp.bfloat16), grad_out.astype(jnp.bfloat16), row_grads, dots

    w_in_grad, w_out_grad, row_grads, dots = lax.map(one_expert, (
        buf_in.reshape(EXPERTS, buffer_rows, D_SUB), buf_cot.reshape(EXPERTS, buffer_rows, D_SUB),
        buf_gate.reshape(EXPERTS, buffer_rows), w_in, w_out))
    pair_grads = row_grads.reshape(total, D_SUB)[target].reshape(devices * local_rows, 2, D_SUB)
    input_grad = jnp.sum(pair_grads, axis=1).astype(jnp.bfloat16).reshape(TOKENS, HEADS * D_SUB)
    gate_grad = dots.reshape(total)[target].reshape(SUBTOK, 2)
    return input_grad, gate_grad, w_in_grad, w_out_grad
```

```python
import functools

import jax
import jax.numpy as jnp
from jax import lax
from jax.experimental import pallas as pl
from jax.experimental.pallas import tpu as pltpu
from jax.sharding import PartitionSpec as P

MESH = pl.DeviceIdType.MESH
F32 = jnp.float32
BF16 = jnp.bfloat16

HEADS = 4
WIDTH = 1024
HID = 1024
TOK = 32
ROWS = 128
NE = 128
CAP = 4
CHUNKS = 4
CH = NE // CHUNKS
GROUP = 16
CROWS = CH * CAP
SIZES = (8, 4, 4)


def offsets(k):
    dz = (k * 5) & 7
    rest = k >> 3
    dx = (rest + dz) & 3
    dy = ((rest >> 2) + (dz >> 1)) & 3
    return dz, dy, dx


def partner(me, k, sign):
    z, y, x = me >> 4, (me >> 2) & 3, me & 3
    dz, dy, dx = offsets(k)
    return (
        ((z + sign * dz + 8) & 7) * 16 + ((y + sign * dy + 4) & 3) * 4 + ((x + sign * dx + 4) & 3)
    )


def iota(shape, axis):
    return lax.broadcasted_iota(jnp.int32, shape, axis)


def dot(a, b, contract=((1,), (0,)), precision=None):
    return lax.dot_general(
        a, b, (contract, ((), ())), precision=precision, preferred_element_type=F32
    )


def kernel(
    routes_ref,
    gates_ref,
    x_ref,
    g_ref,
    win_hbm,
    wout_hbm,
    dx_out,
    gate_out,
    gin_out,
    gout_out,
    win,
    wout,
    table,
    stacked,
    hits,
    send,
    recv,
    recv2,
    back,
    ret,
    dsend,
    dret,
    psend,
    precv,
    pdsend,
    pdrecv,
    xs,
    ss,
    act,
    dhid,
    gin,
    gout,
    gin16,
    gout16,
    acc,
    w_sem,
    send_sem,
    recv_sem,
    fsend_sem,
    frecv_sem,
    bsend_sem,
    brecv_sem,
    dsend_sem,
    drecv_sem,
    psend_sem,
    precv_sem,
    pdsend_sem,
    pdrecv_sem,
    o_sem,
):
    dp = lax.axis_index("dp")
    me = lax.axis_index("expert")
    other = 1 - dp

    barrier = pltpu.get_barrier_semaphore()

    def greet(k, carry):
        pl.semaphore_signal(
            barrier, inc=1, device_id=(dp, partner(me, k, -1)), device_id_type=MESH
        )
        return carry

    lax.fori_loop(1, NE, greet, 0)
    pl.semaphore_signal(barrier, inc=1, device_id=(other, me), device_id_type=MESH)

    load_in = pltpu.make_async_copy(win_hbm, win, w_sem.at[0])
    load_out = pltpu.make_async_copy(wout_hbm, wout, w_sem.at[1])
    load_in.start()
    load_out.start()

    for h in range(HEADS):
        for part in range(2):
            at = h * WIDTH + part * 512
            stacked[pl.ds(part * ROWS + h * TOK, TOK), :] = x_ref[:, at : at + 512]
            stacked[pl.ds((2 + part) * ROWS + h * TOK, TOK), :] = g_ref[:, at : at + 512]
    table[...] = jnp.zeros_like(table)
    table[0:2, :] = routes_ref[...].astype(F32)
    table[2:4, :] = gates_ref[...].astype(F32)
    row, col = iota((ROWS, ROWS), 0), iota((ROWS, ROWS), 1)
    number_of_row, number_of_col = (row & 31) * 4 + (row >> 5), (col & 31) * 4 + (col >> 5)
    reorder = (row == number_of_col).astype(F32).astype(BF16)
    earlier = (number_of_row < number_of_col).astype(F32).astype(BF16)
    own = dot(table[...].astype(BF16), reorder)
    r0, r1, g0, g1 = own[0:1], own[1:2], own[2:3], own[3:4]

    pl.semaphore_wait(barrier, NE)

    def place(j, carry):
        shape = (CH * 16, ROWS)
        line = iota(shape, 0)
        expert = partner(me, j * CH + (line >> 4), 1).astype(F32)
        first, second = expert == r0, expert == r1
        member = jnp.where(first | second, 1.0, 0.0)
        count = dot(member.astype(BF16), earlier)
        slot = (line & 3).astype(F32)
        hit = jnp.where(count == slot, member, 0.0)
        gated = hit * jnp.where(first, g0, g1)
        part = (line >> 2) & 3
        hits[j] = hit.T.astype(BF16)
        spread = jnp.concatenate(
            [
                jnp.where(part == p, hit if p < 2 else gated, 0.0).astype(BF16) for p in range(4)
            ],
            axis=1,
        )
        rows = dot(spread, stacked[...]).astype(BF16)
        send[pl.ds(j * CH, CH)] = rows.reshape(CH, 16, 512)

        @pl.when(j == 0)
        def _():
            pltpu.make_async_copy(send.at[0], recv.at[0], recv_sem.at[0]).start()

        def push(i, c):
            k = j * CH + i
            pltpu.make_async_remote_copy(
                send.at[k],
                recv.at[k],
                send_sem,
                recv_sem.at[j],
                device_id=(dp, partner(me, k, 1)),
                device_id_type=MESH,
            ).start()
            return c

        lax.fori_loop(jnp.where(j == 0, 1, 0), CH, push, 0)
        return carry

    lax.fori_loop(0, CHUNKS, place, 0)

    gin[...] = jnp.zeros_like(gin)
    gout[...] = jnp.zeros_like(gout)
    acc[...] = jnp.zeros_like(acc)
    load_in.wait()
    load_out.wait()

    size = GROUP * 16
    to, frm = iota((size, size), 0), iota((size, size), 1)
    unpack = (
        (frm == ((to & 63) >> 2) * 16 + (to >> 6) * 4 + (to & 3)).astype(F32).astype(BF16)
    )
    pack = (to == ((frm & 63) >> 2) * 16 + (frm >> 6) * 4 + (frm & 3)).astype(F32).astype(BF16)

    def open_rows(source, j, base):
        for b in range(CH // GROUP):
            raw = source[pl.ds(j * CH + b * GROUP, GROUP)].reshape(size, 512)
            rows = dot(unpack, raw).astype(BF16)
            at = base + b * 64
            xs[at : at + 64, 0:512] = rows[0:64]
            xs[at : at + 64, 512:1024] = rows[64:128]
            ss[at : at + 64, 0:512] = rows[128:192]
            ss[at : at + 64, 512:1024] = rows[192:256]

    def step(j, carry):
        mine = pl.ds(j * CH, CH)
        pltpu.make_async_copy(recv.at[mine], recv.at[mine], recv_sem.at[j]).wait()
        forward = pltpu.make_async_remote_copy(
            recv.at[mine],
            recv2.at[mine],
            fsend_sem.at[j],
            frecv_sem.at[j],
            device_id=(other, me),
            device_id_type=MESH,
        )
        forward.start()
        open_rows(recv, j, 0)
        forward.wait_recv()
        open_rows(recv2, j, CROWS)

        dots = jnp.zeros((2 * CROWS, 1), F32)
        for b in range(HID // 256):
            cols = slice(b * 256, b * 256 + 256)
            hidden = dot(xs[...], win[:, cols])
            pulled = dot(ss[...], wout[cols, :], ((1,), (1,)))
            square = hidden * hidden
            tangent = jnp.tanh(0.7978845608028654 * (hidden + 0.044715 * square * hidden))
            active = (0.5 * hidden * (1.0 + tangent)).astype(BF16)
            slope = 0.5 * (1.0 + tangent) + 0.5 * hidden * (
                1.0 - tangent * tangent
            ) * 0.7978845608028654 * (1.0 + 3.0 * 0.044715 * square)
            act[:, cols] = active
            dhid[:, cols] = (pulled * slope).astype(BF16)
            dots = dots + jnp.sum(active.astype(F32) * pulled, axis=1, keepdims=True)
        partial = dot(dhid[...], win[...], ((1,), (1,)))
        psend[j] = partial[CROWS:].astype(BF16)
        wide = jnp.broadcast_to(dots, (2 * CROWS, 128))
        pdsend[j] = wide[CROWS:]
        swap = pltpu.make_async_remote_copy(
            psend.at[j],
            precv.at[j],
            psend_sem.at[j],
            precv_sem.at[j],
            device_id=(other, me),
            device_id_type=MESH,
        )
        swap_dots = pltpu.make_async_remote_copy(
            pdsend.at[j],
            pdrecv.at[j],
            pdsend_sem.at[j],
            pdrecv_sem.at[j],
            device_id=(other, me),
            device_id_type=MESH,
        )
        swap.start()
        swap_dots.start()
        for b in range(HID // 256):
            cols = slice(b * 256, b * 256 + 256)
            gout[cols, :] += dot(act[:, cols], ss[...], ((0,), (0,)))
            gin[cols, :] += dot(xs[:, cols], dhid[...], ((0,), (0,)))
        swap.wait_recv()
        swap_dots.wait_recv()
        whole = (partial[:CROWS] + precv[j].astype(F32)).astype(BF16)
        for b in range(CH // GROUP):
            rows = whole[b * 64 : b * 64 + 64]
            tall = jnp.concatenate([rows[:, p * 256 : p * 256 + 256] for p in range(4)], axis=0)
            back[pl.ds(j * CH + b * GROUP, GROUP)] = (
                dot(pack, tall).astype(BF16).reshape(GROUP, 16, 256)
            )
        all_dots = wide[:CROWS] + pdrecv[j]
        line, lane = iota((CROWS, 128), 0), iota((CROWS, 128), 1)
        spread = jnp.where((line & 3) == lane, all_dots, 0.0)
        gather = (iota((CH, CROWS), 0) == (iota((CH, CROWS), 1) >> 2)).astype(F32)
        dsend[mine] = dot(gather, spread, precision=lax.Precision.HIGHEST).reshape(CH, 1, 128)

        @pl.when(j == 0)
        def _():
            pltpu.make_async_copy(back.at[0], ret.at[0], brecv_sem.at[0]).start()
            pltpu.make_async_copy(dsend.at[0], dret.at[0], drecv_sem.at[0]).start()

        def push(i, c):
            k = j * CH + i
            target = (dp, partner(me, k, -1))
            pltpu.make_async_remote_copy(
                back.at[k],
                ret.at[k],
                bsend_sem,
                brecv_sem.at[j],
                device_id=target,
                device_id_type=MESH,
            ).start()
            pltpu.make_async_remote_copy(
                dsend.at[k],
                dret.at[k],
                dsend_sem,
                drecv_sem.at[j],
                device_id=target,
                device_id_type=MESH,
            ).start()
            return c

        lax.fori_loop(jnp.where(j == 0, 1, 0), CH, push, 0)
        return carry

    lax.fori_loop(0, CHUNKS, step, 0)

    gin16[...] = gin[...].astype(BF16)
    gout16[...] = gout[...].astype(BF16)
    store_in = pltpu.make_async_copy(gin16, gin_out, o_sem.at[0])
    store_out = pltpu.make_async_copy(gout16, gout_out, o_sem.at[1])
    store_in.start()
    store_out.start()

    def collect(j, carry):
        mine = pl.ds(j * CH, CH)
        pltpu.make_async_copy(ret.at[mine], ret.at[mine], brecv_sem.at[j]).wait()
        lane = iota((ROWS, CH * 16), 1)
        hit = hits[j].astype(F32)
        picks = jnp.concatenate(
            [jnp.where(((lane >> 2) & 3) == q, hit, 0.0).astype(BF16) for q in range(4)], axis=0
        )
        acc[...] += dot(picks, ret[mine].reshape(CH * 16, 256))
        return carry

    lax.fori_loop(0, CHUNKS, collect, 0)
    for h in range(HEADS):
        for q in range(4):
            at = h * WIDTH + q * 256
            dx_out[:, at : at + 256] = acc[
                q * ROWS + h * TOK : q * ROWS + h * TOK + TOK, :
            ].astype(BF16)

    for j in range(CHUNKS):
        mine = pl.ds(j * CH, CH)
        pltpu.make_async_copy(dret.at[mine], dret.at[mine], drecv_sem.at[j]).wait()
    values = dret[...].reshape(NE, 128)
    expert = partner(me, iota((NE, ROWS), 0), 1).astype(F32)
    n0, n1 = table[0:1], table[1:2]
    first, second = expert == n0, expert == n1
    member = jnp.where(first | second, 1.0, 0.0)
    before = (row < col).astype(F32).astype(BF16)
    count = dot(member.astype(BF16), before)
    picked = jnp.zeros((NE, ROWS), F32)
    for s in range(CAP):
        picked = picked + jnp.where(count == float(s), values[:, s : s + 1], 0.0)
    gate_out[0:1, :] = (
        jnp.sum(jnp.where(first, picked, 0.0), axis=0, keepdims=True) / table[2:3]
    )
    gate_out[1:2, :] = (
        jnp.sum(jnp.where(second, picked, 0.0), axis=0, keepdims=True) / table[3:4]
    )

    rest = pl.ds(1, NE - 1)
    pltpu.make_async_copy(send.at[rest], send.at[rest], send_sem).wait()
    pltpu.make_async_copy(back.at[rest], back.at[rest], bsend_sem).wait()
    pltpu.make_async_copy(dsend.at[rest], dsend.at[rest], dsend_sem).wait()
    for j in range(CHUNKS):
        mine = pl.ds(j * CH, CH)
        pltpu.make_async_copy(recv.at[mine], recv.at[mine], fsend_sem.at[j]).wait()
        pltpu.make_async_copy(psend.at[j], psend.at[j], psend_sem.at[j]).wait()
        pltpu.make_async_copy(pdsend.at[j], pdsend.at[j], pdsend_sem.at[j]).wait()
    store_in.wait()
    store_out.wait()


def body(inputs, cotangent, gates, routes, w_in, w_out):
    vmem, hbm = pl.BlockSpec(memory_space=pltpu.VMEM), pl.BlockSpec(memory_space=pl.ANY)
    dma = pltpu.SemaphoreType.DMA
    dx, gate, gin, gout = pl.pallas_call(
        kernel,
        out_shape=(
            jax.ShapeDtypeStruct(inputs.shape, BF16),
            jax.ShapeDtypeStruct((2, ROWS), F32),
            jax.ShapeDtypeStruct((WIDTH, HID), BF16),
            jax.ShapeDtypeStruct((HID, WIDTH), BF16),
        ),
        in_specs=[vmem, vmem, vmem, vmem, hbm, hbm],
        out_specs=(vmem, vmem, hbm, hbm),
        scratch_shapes=[
            pltpu.VMEM((WIDTH, HID), BF16),
            pltpu.VMEM((HID, WIDTH), BF16),
            pltpu.VMEM((8, ROWS), F32),
            pltpu.VMEM((4 * ROWS, 512), BF16),
            pltpu.VMEM((CHUNKS, ROWS, CH * 16), BF16),
            pltpu.VMEM((NE, 16, 512), BF16),
            pltpu.VMEM((NE, 16, 512), BF16),
            pltpu.VMEM((NE, 16, 512), BF16),
            pltpu.VMEM((NE, 16, 256), BF16),
            pltpu.VMEM((NE, 16, 256), BF16),
            pltpu.VMEM((NE, 1, 128), F32),
            pltpu.VMEM((NE, 1, 128), F32),
            pltpu.VMEM((CHUNKS, CROWS, WIDTH), BF16),
            pltpu.VMEM((CHUNKS, CROWS, WIDTH), BF16),
            pltpu.VMEM((CHUNKS, CROWS, 128), F32),
            pltpu.VMEM((CHUNKS, CROWS, 128), F32),
            pltpu.VMEM((2 * CROWS, WIDTH), BF16),
            pltpu.VMEM((2 * CROWS, WIDTH), BF16),
            pltpu.VMEM((2 * CROWS, HID), BF16),
            pltpu.VMEM((2 * CROWS, HID), BF16),
            pltpu.VMEM((WIDTH, HID), F32),
            pltpu.VMEM((HID, WIDTH), F32),
            pltpu.VMEM((WIDTH, HID), BF16),
            pltpu.VMEM((HID, WIDTH), BF16),
            pltpu.VMEM((4 * ROWS, 256), F32),
            dma((2,)),
            dma,
            dma((CHUNKS,)),
            dma((CHUNKS,)),
            dma((CHUNKS,)),
            dma,
            dma((CHUNKS,)),
            dma,
            dma((CHUNKS,)),
            dma((CHUNKS,)),
            dma((CHUNKS,)),
            dma((CHUNKS,)),
            dma((CHUNKS,)),
            dma((2,)),
        ],
        compiler_params=pltpu.CompilerParams(
            collective_id=0, has_side_effects=True, vmem_limit_bytes=56 << 20
        ),
        name="experts",
    )(routes.T, gates.T, inputs, cotangent, w_in[0], w_out[0])
    return dx, gate.T, gin[None], gout[None]


def solution(mesh):
    return jax.shard_map(
        body,
        mesh=mesh,
        in_specs=(
            P(("dp", "expert"), None),
            P(("dp", "expert"), None),
            P(("dp", "expert"), None),
            P(("dp", "expert"), None),
            P("expert", None, "dp"),
            P("expert", "dp", None),
        ),
        out_specs=(
            P(("dp", "expert"), None),
            P(("dp", "expert"), None),
            P("expert", None, "dp"),
            P("expert", "dp", None),
        ),
        check_vma=False,
    )
```

```python
import functools

import jax
import jax.numpy as jnp
from jax import lax
from jax.experimental import pallas as pl
from jax.experimental.pallas import tpu as pltpu
from jax.sharding import PartitionSpec as P

MESH = pl.DeviceIdType.MESH
F32 = jnp.float32
BF16 = jnp.bfloat16

HEADS = 4
WIDTH = 1024
HID = 1024
TOK = 32
ROWS = 128
NE = 128
CAP = 4
CHUNKS = 4
CH = NE // CHUNKS
GROUP = 16
CROWS = CH * CAP
SIZES = (8, 4, 4)


def offsets(k):
    plane, place = k >> 4, k & 15
    dz = (4 - (plane >> 1)) * (1 - 2 * (plane & 1)) + 4 * (1 - ((plane + 7) >> 3))
    return dz, place >> 2, place & 3


def partner(me, k, sign, lift=0):
    z, y, x = me >> 4, (me >> 2) & 3, me & 3
    dz, dy, dx = offsets(k)
    return (
        ((z + sign * dz + lift + 16) & 7) * 16
        + ((y + sign * dy + 4) & 3) * 4
        + ((x + sign * dx + 4) & 3)
    )


def iota(shape, axis):
    return lax.broadcasted_iota(jnp.int32, shape, axis)


def dot(a, b, contract=((1,), (0,)), precision=None):
    return lax.dot_general(
        a, b, (contract, ((), ())), precision=precision, preferred_element_type=F32
    )


def kernel(
    routes_hbm,
    gates_hbm,
    x_hbm,
    g_hbm,
    win_hbm,
    wout_hbm,
    dx_out,
    gate_out,
    gin_out,
    gout_out,
    win,
    wout,
    routes_ref,
    gates_ref,
    x_ref,
    g_ref,
    raw_table,
    table,
    stack_x,
    stack_g,
    near_table,
    near_x,
    near_g,
    near_stack_x,
    near_stack_g,
    hits,
    plan_x,
    plan_s,
    send_x,
    send_s,
    recv_x,
    recv_s,
    recv2_x,
    recv2_s,
    back,
    ret,
    dsend,
    dret,
    psend,
    precv,
    pdsend,
    pdrecv,
    xs,
    ss,
    act,
    dhid,
    gin,
    gout,
    acc,
    w_sem,
    line_sem,
    t_send,
    t_recv,
    send_sem,
    rx_sem,
    rs_sem,
    fsend_sem,
    fx_sem,
    fs_sem,
    bsend_sem,
    brecv_sem,
    dsend_sem,
    drecv_sem,
    psend_sem,
    precv_sem,
    pdsend_sem,
    pdrecv_sem,
):
    dp = lax.axis_index("dp")
    me = lax.axis_index("expert")
    other = 1 - dp
    loads = [
        pltpu.make_async_copy(source, target, w_sem.at[2 + n])
        for n, (source, target) in enumerate(
            ((routes_hbm, routes_ref), (gates_hbm, gates_ref), (x_hbm, x_ref), (g_hbm, g_ref))
        )
    ]
    for load in loads:
        load.start()

    barrier = pltpu.get_barrier_semaphore()

    def along(axis, step):
        z, y, x = me >> 4, (me >> 2) & 3, me & 3
        if axis == 0:
            z = (z + step) & 7
        elif axis == 1:
            y = (y + step) & 3
        else:
            x = (x + step) & 3
        return (dp, z * 16 + y * 4 + x)

    def greet(semaphore, axis):
        for step in (1, 7, 2, 6, 3, 5, 4) if axis == 0 else (1, 3, 2):
            pl.semaphore_signal(
                semaphore, inc=1, device_id=along(axis, step), device_id_type=MESH
            )

    for axis in range(3):
        greet(barrier, axis)
    pl.semaphore_signal(barrier, inc=1, device_id=(other, me), device_id_type=MESH)
    pl.semaphore_wait(barrier, 14)

    def hand(n, source, target):
        copies = []
        for side in range(2):
            copy = pltpu.make_async_remote_copy(
                source,
                target.at[side],
                t_send.at[n, side],
                t_recv.at[n, side],
                device_id=along(0, 1 - 2 * side),
                device_id_type=MESH,
            )
            copy.start()
            copies.append(copy)
        return copies

    hand_x = hand(1, x_hbm, near_x)
    greet(line_sem.at[0], 1)

    row, col = iota((ROWS, ROWS), 0), iota((ROWS, ROWS), 1)
    number_of_row, number_of_col = (row & 31) * 4 + (row >> 5), (col & 31) * 4 + (col >> 5)
    reorder = (row == number_of_col).astype(F32).astype(BF16)
    earlier = (number_of_row < number_of_col).astype(F32).astype(BF16)
    raw_table[...] = jnp.zeros_like(raw_table)
    loads[0].wait()
    loads[1].wait()
    raw_table[0:2, :] = routes_ref[...].astype(F32)
    raw_table[2:4, :] = gates_ref[...].astype(F32)
    table[...] = dot(raw_table[...].astype(BF16), reorder)
    hand_table = hand(0, table, near_table)
    hand_g = hand(2, g_hbm, near_g)

    def stack(source, target):
        for h in range(HEADS):
            for part in range(4):
                at = h * WIDTH + part * 256
                target[pl.ds(part * ROWS + h * TOK, TOK), :] = source[:, at : at + 256]

    pl.semaphore_wait(line_sem.at[0], 3)
    greet(line_sem.at[1], 2)

    def chosen(source, lines, first_line, origin, base):
        shape = (lines, ROWS)
        line = iota(shape, 0) + first_line
        expert = partner(origin, base + (line >> 4), 1).astype(F32)
        first, second = expert == source[0:1], expert == source[1:2]
        member = jnp.where(first | second, 1.0, 0.0)
        count = dot(member.astype(BF16), earlier)
        hit = jnp.where(count == (line & 3).astype(F32), member, 0.0)
        return line, first, hit

    def plan(unit, source, lines, first_line, origin, base):
        line, first, hit = chosen(source, lines, first_line, origin, base)
        gated = hit * jnp.where(first, source[2:3], source[3:4])
        part = (line >> 2) & 3
        at = pl.ds(first_line, lines)
        for p in range(4):
            cols = slice(p * ROWS, p * ROWS + ROWS)
            plan_x[unit, at, cols] = jnp.where(part == p, hit, 0.0).astype(BF16)
            plan_s[unit, at, cols] = jnp.where(part == p, gated, 0.0).astype(BF16)

    def place(unit, plans, stacks, sends, recvs, sems, side):
        base, start, stop = unit * 16, 0, 16
        if unit == 1:
            start, stop = side * 8, side * 8 + 8
        tokens = stacks if side is None else stacks.at[side]
        lines = slice(start * 16, stop * 16)
        made = dot(plans[unit, lines, :], tokens[...]).astype(BF16)
        sends[base + start : base + stop] = made.reshape(stop - start, 16, 256)
        lift = 0 if side is None else (-1, 1)[side]
        sem = sems.at[unit // 2]
        if unit in (0, 6, 7):
            pltpu.make_async_copy(sends.at[base], recvs.at[base], sem).start()
            start = 1

        def push(i, carry):
            k = base + i
            pltpu.make_async_remote_copy(
                sends.at[k],
                recvs.at[k],
                send_sem,
                sem,
                device_id=(dp, partner(me, k, 1, lift)),
                device_id_type=MESH,
            ).start()
            return carry

        lax.fori_loop(start, stop, push, 0)

    plan(0, table[...], 256, 0, me, 0)
    loads[2].wait()
    loads[3].wait()
    stack(x_ref, stack_x)
    stack(g_ref, stack_g)
    pl.semaphore_wait(line_sem.at[1], 3)
    place(0, plan_x, stack_x, send_x, recv_x, rx_sem, None)
    place(0, plan_s, stack_g, send_s, recv_s, rs_sem, None)
    for side in range(2):
        hand_table[side].wait_recv()
    origins = (along(0, -1)[1], along(0, 1)[1])
    units = ((1, 0), (1, 1), (2, 0), (3, 1), (6, 0), (7, 1), (4, 0), (5, 1))
    for unit, side in units:
        lines, first_line = (128, 128 * side) if unit == 1 else (256, 0)
        plan(unit, near_table[side], lines, first_line, origins[side], unit * 16)
    for side in range(2):
        hand_x[side].wait_recv()
        stack(near_x.at[side], near_stack_x.at[side])
    for unit, side in units:
        place(unit, plan_x, near_stack_x, send_x, recv_x, rx_sem, side)
    for side in range(2):
        hand_g[side].wait_recv()
        stack(near_g.at[side], near_stack_g.at[side])
    for unit, side in units:
        place(unit, plan_s, near_stack_g, send_s, recv_s, rs_sem, side)

    load_in = pltpu.make_async_copy(win_hbm, win, w_sem.at[0])
    load_out = pltpu.make_async_copy(wout_hbm, wout, w_sem.at[1])
    load_in.start()
    load_out.start()

    def remember(j, carry):
        _, _, hit = chosen(table[...], CH * 16, 0, me, j * CH)
        hits[j] = hit.T.astype(BF16)
        return carry

    lax.fori_loop(0, CHUNKS, remember, 0)
    gin[...] = jnp.zeros_like(gin)
    gout[...] = jnp.zeros_like(gout)
    acc[...] = jnp.zeros_like(acc)
    load_in.wait()
    load_out.wait()

    size = GROUP * 16
    to, frm = iota((size, size), 0), iota((size, size), 1)
    unpack = (
        (frm == ((to & 63) >> 2) * 16 + (to >> 6) * 4 + (to & 3)).astype(F32).astype(BF16)
    )
    pack = (to == ((frm & 63) >> 2) * 16 + (frm >> 6) * 4 + (frm & 3)).astype(F32).astype(BF16)

    def open_rows(source, target, j, base):
        for b in range(CH // GROUP):
            raw = source[pl.ds(j * CH + b * GROUP, GROUP)].reshape(size, 256)
            rows = dot(unpack, raw).astype(BF16)
            at = base + b * 64
            for p in range(4):
                target[at : at + 64, p * 256 : p * 256 + 256] = rows[p * 64 : p * 64 + 64]

    def step(j, carry):
        mine = pl.ds(j * CH, CH)
        forwards = []
        for n, (got, passed, sem, fsem) in enumerate(
            ((recv_x, recv2_x, rx_sem, fx_sem), (recv_s, recv2_s, rs_sem, fs_sem))
        ):
            pltpu.make_async_copy(got.at[mine], got.at[mine], sem.at[j]).wait()
            forward = pltpu.make_async_remote_copy(
                got.at[mine],
                passed.at[mine],
                fsend_sem.at[n, j],
                fsem.at[j],
                device_id=(other, me),
                device_id_type=MESH,
            )
            forward.start()
            forwards.append(forward)
            open_rows(got, (xs, ss)[n], j, 0)
        forwards[0].wait_recv()
        open_rows(recv2_x, xs, j, CROWS)
        forwards[1].wait_recv()
        open_rows(recv2_s, ss, j, CROWS)

        dots = jnp.zeros((2 * CROWS, 1), F32)
        for b in range(HID // 256):
            cols = slice(b * 256, b * 256 + 256)
            hidden = dot(xs[...], win[:, cols])
            pulled = dot(ss[...], wout[cols, :], ((1,), (1,)))
            square = hidden * hidden
            tangent = jnp.tanh(0.7978845608028654 * (hidden + 0.044715 * square * hidden))
            active = (0.5 * hidden * (1.0 + tangent)).astype(BF16)
            slope = 0.5 * (1.0 + tangent) + 0.5 * hidden * (
                1.0 - tangent * tangent
            ) * 0.7978845608028654 * (1.0 + 3.0 * 0.044715 * square)
            act[:, cols] = active
            dhid[:, cols] = (pulled * slope).astype(BF16)
            dots = dots + jnp.sum(active.astype(F32) * pulled, axis=1, keepdims=True)
        partial = dot(dhid[...], win[...], ((1,), (1,)))
        psend[j] = partial[CROWS:].astype(BF16)
        wide = jnp.broadcast_to(dots, (2 * CROWS, 128))
        pdsend[j] = wide[CROWS:]
        swap = pltpu.make_async_remote_copy(
            psend.at[j],
            precv.at[j],
            psend_sem.at[j],
            precv_sem.at[j],
            device_id=(other, me),
            device_id_type=MESH,
        )
        swap_dots = pltpu.make_async_remote_copy(
            pdsend.at[j],
            pdrecv.at[j],
            pdsend_sem.at[j],
            pdrecv_sem.at[j],
            device_id=(other, me),
            device_id_type=MESH,
        )
        swap.start()
        swap_dots.start()
        for b in range(HID // 256):
            cols = slice(b * 256, b * 256 + 256)
            gout[cols, :] += dot(act[:, cols], ss[...], ((0,), (0,)))
            gin[cols, :] += dot(xs[:, cols], dhid[...], ((0,), (0,)))
        swap.wait_recv()
        swap_dots.wait_recv()
        whole = (partial[:CROWS] + precv[j].astype(F32)).astype(BF16)
        for b in range(CH // GROUP):
            rows = whole[b * 64 : b * 64 + 64]
            tall = jnp.concatenate([rows[:, p * 256 : p * 256 + 256] for p in range(4)], axis=0)
            back[pl.ds(j * CH + b * GROUP, GROUP)] = (
                dot(pack, tall).astype(BF16).reshape(GROUP, 16, 256)
            )
        all_dots = wide[:CROWS] + pdrecv[j]
        line, lane = iota((CROWS, 128), 0), iota((CROWS, 128), 1)
        spread = jnp.where((line & 3) == lane, all_dots, 0.0)
        gather = (iota((CH, CROWS), 0) == (iota((CH, CROWS), 1) >> 2)).astype(F32)
        dsend[mine] = dot(gather, spread, precision=lax.Precision.HIGHEST).reshape(CH, 1, 128)

        @pl.when(j == 0)
        def _():
            pltpu.make_async_copy(back.at[0], ret.at[0], brecv_sem.at[0]).start()
            pltpu.make_async_copy(dsend.at[0], dret.at[0], drecv_sem.at[0]).start()

        def push(i, c):
            k = j * CH + i
            target = (dp, partner(me, k, -1))
            pltpu.make_async_remote_copy(
                back.at[k],
                ret.at[k],
                bsend_sem,
                brecv_sem.at[j],
                device_id=target,
                device_id_type=MESH,
            ).start()
            pltpu.make_async_remote_copy(
                dsend.at[k],
                dret.at[k],
                dsend_sem,
                drecv_sem.at[j],
                device_id=target,
                device_id_type=MESH,
            ).start()
            return c

        lax.fori_loop(jnp.where(j == 0, 1, 0), CH, push, 0)
        return carry

    lax.fori_loop(0, CHUNKS, step, 0)

    gin_out[...] = gin[...].astype(BF16)
    gout_out[...] = gout[...].astype(BF16)

    expert = partner(me, iota((NE, ROWS), 0), 1).astype(F32)
    n0, n1 = raw_table[0:1], raw_table[1:2]
    first, second = expert == n0, expert == n1
    member = jnp.where(first | second, 1.0, 0.0)
    before = (row < col).astype(F32).astype(BF16)
    count = dot(member.astype(BF16), before)

    def collect(j, carry):
        mine = pl.ds(j * CH, CH)
        lane = iota((ROWS, CH * 16), 1)
        hit = hits[j].astype(F32)
        picks = jnp.concatenate(
            [jnp.where(((lane >> 2) & 3) == q, hit, 0.0).astype(BF16) for q in range(4)], axis=0
        )
        pltpu.make_async_copy(ret.at[mine], ret.at[mine], brecv_sem.at[j]).wait()
        acc[...] += dot(picks, ret[mine].reshape(CH * 16, 256))
        return carry

    lax.fori_loop(0, CHUNKS, collect, 0)
    for h in range(HEADS):
        for q in range(4):
            at = h * WIDTH + q * 256
            dx_out[:, at : at + 256] = acc[
                q * ROWS + h * TOK : q * ROWS + h * TOK + TOK, :
            ].astype(BF16)

    for j in range(CHUNKS):
        mine = pl.ds(j * CH, CH)
        pltpu.make_async_copy(dret.at[mine], dret.at[mine], drecv_sem.at[j]).wait()
    values = dret[...].reshape(NE, 128)
    picked = jnp.zeros((NE, ROWS), F32)
    for s in range(CAP):
        picked = picked + jnp.where(count == float(s), values[:, s : s + 1], 0.0)
    gate_out[0:1, :] = (
        jnp.sum(jnp.where(first, picked, 0.0), axis=0, keepdims=True) / raw_table[2:3]
    )
    gate_out[1:2, :] = (
        jnp.sum(jnp.where(second, picked, 0.0), axis=0, keepdims=True) / raw_table[3:4]
    )

    rest = pl.ds(1, NE - 1)
    for copy in hand_table + hand_x + hand_g:
        copy.wait_send()
    sent = pl.ds(3, NE - 3)
    pltpu.make_async_copy(send_x.at[sent], send_x.at[sent], send_sem).wait()
    pltpu.make_async_copy(send_s.at[sent], send_s.at[sent], send_sem).wait()
    pltpu.make_async_copy(back.at[rest], back.at[rest], bsend_sem).wait()
    pltpu.make_async_copy(dsend.at[rest], dsend.at[rest], dsend_sem).wait()
    for j in range(CHUNKS):
        mine = pl.ds(j * CH, CH)
        pltpu.make_async_copy(recv_x.at[mine], recv_x.at[mine], fsend_sem.at[0, j]).wait()
        pltpu.make_async_copy(recv_s.at[mine], recv_s.at[mine], fsend_sem.at[1, j]).wait()
        pltpu.make_async_copy(psend.at[j], psend.at[j], psend_sem.at[j]).wait()
        pltpu.make_async_copy(pdsend.at[j], pdsend.at[j], pdsend_sem.at[j]).wait()


def flush(dx, gate, gin, gout, dx_out, gate_out, gin_out, gout_out, sems):
    copies = [
        pltpu.make_async_copy(source, target, sems.at[n])
        for n, (source, target) in enumerate(
            ((gin, gin_out), (gout, gout_out), (dx, dx_out), (gate, gate_out))
        )
    ]
    for copy in copies:
        copy.start()
    for copy in copies:
        copy.wait()


def body(inputs, cotangent, gates, routes, w_in, w_out):
    vmem, hbm = pl.BlockSpec(memory_space=pltpu.VMEM), pl.BlockSpec(memory_space=pl.ANY)
    dma = pltpu.SemaphoreType.DMA
    shapes = (
        (inputs.shape, BF16),
        ((2, ROWS), F32),
        ((WIDTH, HID), BF16),
        ((HID, WIDTH), BF16),
    )
    outs = pl.pallas_call(
        kernel,
        out_shape=tuple(pltpu.VMEM(shape, kind) for shape, kind in shapes),
        in_specs=[hbm] * 6,
        out_specs=(vmem,) * 4,
        scratch_shapes=[
            pltpu.VMEM((WIDTH, HID), BF16),
            pltpu.VMEM((HID, WIDTH), BF16),
            pltpu.VMEM(routes.shape[::-1], jnp.int32),
            pltpu.VMEM(gates.shape[::-1], BF16),
            pltpu.VMEM(inputs.shape, BF16),
            pltpu.VMEM(inputs.shape, BF16),
            pltpu.VMEM((8, ROWS), F32),
            pltpu.VMEM((8, ROWS), F32),
            pltpu.VMEM((4 * ROWS, 256), BF16),
            pltpu.VMEM((4 * ROWS, 256), BF16),
            pltpu.VMEM((2, 8, ROWS), F32),
            pltpu.VMEM((2,) + inputs.shape, BF16),
            pltpu.VMEM((2,) + inputs.shape, BF16),
            pltpu.VMEM((2, 4 * ROWS, 256), BF16),
            pltpu.VMEM((2, 4 * ROWS, 256), BF16),
            pltpu.VMEM((CHUNKS, ROWS, CH * 16), BF16),
            pltpu.VMEM((8, 256, 4 * ROWS), BF16),
            pltpu.VMEM((8, 256, 4 * ROWS), BF16),
            pltpu.VMEM((NE, 16, 256), BF16),
            pltpu.VMEM((NE, 16, 256), BF16),
            pltpu.VMEM((NE, 16, 256), BF16),
            pltpu.VMEM((NE, 16, 256), BF16),
            pltpu.VMEM((NE, 16, 256), BF16),
            pltpu.VMEM((NE, 16, 256), BF16),
            pltpu.VMEM((NE, 16, 256), BF16),
            pltpu.VMEM((NE, 16, 256), BF16),
            pltpu.VMEM((NE, 1, 128), F32),
            pltpu.VMEM((NE, 1, 128), F32),
            pltpu.VMEM((CHUNKS, CROWS, WIDTH), BF16),
            pltpu.VMEM((CHUNKS, CROWS, WIDTH), BF16),
            pltpu.VMEM((CHUNKS, CROWS, 128), F32),
            pltpu.VMEM((CHUNKS, CROWS, 128), F32),
            pltpu.VMEM((2 * CROWS, WIDTH), BF16),
            pltpu.VMEM((2 * CROWS, WIDTH), BF16),
            pltpu.VMEM((2 * CROWS, HID), BF16),
            pltpu.VMEM((2 * CROWS, HID), BF16),
            pltpu.VMEM((WIDTH, HID), F32),
            pltpu.VMEM((HID, WIDTH), F32),
            pltpu.VMEM((4 * ROWS, 256), F32),
            dma((6,)),
            pltpu.SemaphoreType.REGULAR((2,)),
            dma((3, 2)),
            dma((3, 2)),
            dma,
            dma((CHUNKS,)),
            dma((CHUNKS,)),
            dma((2, CHUNKS)),
            dma((CHUNKS,)),
            dma((CHUNKS,)),
            dma,
            dma((CHUNKS,)),
            dma,
            dma((CHUNKS,)),
            dma((CHUNKS,)),
            dma((CHUNKS,)),
            dma((CHUNKS,)),
            dma((CHUNKS,)),
        ],
        compiler_params=pltpu.CompilerParams(
            collective_id=0, has_side_effects=True, vmem_limit_bytes=48 << 20
        ),
        name="experts",
    )(
        *(
            pltpu.with_memory_space_constraint(array, pltpu.HBM)
            for array in (routes.T, gates.T, inputs, cotangent, w_in[0], w_out[0])
        )
    )
    dx, gate, gin, gout = pl.pallas_call(
        flush,
        out_shape=tuple(jax.ShapeDtypeStruct(shape, kind) for shape, kind in shapes),
        in_specs=[vmem] * 4,
        out_specs=(hbm,) * 4,
        scratch_shapes=[dma((4,))],
        compiler_params=pltpu.CompilerParams(vmem_limit_bytes=1 << 20),
        name="flush",
    )(*outs)
    return dx, gate.T, gin[None], gout[None]


def solution(mesh):
    return jax.shard_map(
        body,
        mesh=mesh,
        in_specs=(
            P(("dp", "expert"), None),
            P(("dp", "expert"), None),
            P(("dp", "expert"), None),
            P(("dp", "expert"), None),
            P("expert", None, "dp"),
            P("expert", "dp", None),
        ),
        out_specs=(
            P(("dp", "expert"), None),
            P(("dp", "expert"), None),
            P("expert", None, "dp"),
            P("expert", "dp", None),
        ),
        check_vma=False,
    )
```

```python
import functools

import jax
import jax.numpy as jnp
from jax import lax
from jax.experimental import pallas as pl
from jax.experimental.pallas import tpu as pltpu
from jax.sharding import PartitionSpec as P

MESH = pl.DeviceIdType.MESH
F32 = jnp.float32
BF16 = jnp.bfloat16

HEADS = 4
WIDTH = 1024
HID = 1024
TOK = 32
ROWS = 128
NE = 128
CAP = 4
CHUNKS = 4
CH = NE // CHUNKS
GROUP = 16
CROWS = CH * CAP
OWN = 4
HALVES = 5


def offsets(k):
    high, low, place = k >> 6, (k >> 5) & 1, k & 15
    second, third, fourth = (1 - high) * low, high * (1 - low), high * low
    dz = (1 + 2 * second - 3 * third + fourth) * (1 - 2 * ((k >> 4) & 1)) + 2 * third
    return dz, place >> 2, place & 3


def partner(me, k, sign, lift=0):
    z, y, x = me >> 4, (me >> 2) & 3, me & 3
    dz, dy, dx = offsets(k)
    return (
        ((z + sign * dz + lift + 16) & 7) * 16
        + ((y + sign * dy + 4) & 3) * 4
        + ((x + sign * dx + 4) & 3)
    )


def iota(shape, axis):
    return lax.broadcasted_iota(jnp.int32, shape, axis)


def dot(a, b, contract=((1,), (0,)), precision=None):
    return lax.dot_general(
        a, b, (contract, ((), ())), precision=precision, preferred_element_type=F32
    )


def kernel(
    routes_hbm,
    gates_hbm,
    x_hbm,
    g_hbm,
    win_hbm,
    wout_hbm,
    dx_out,
    gate_out,
    gin_out,
    gout_out,
    win,
    wout,
    routes_ref,
    gates_ref,
    x_ref,
    g_ref,
    raw_table,
    table,
    stack_x,
    stack_g,
    near_table,
    near_x,
    near_g,
    near_stack_x,
    near_stack_g,
    hits,
    plan_x,
    plan_s,
    send_x,
    send_s,
    recv_x,
    recv_s,
    recv2_x,
    recv2_s,
    back,
    ret,
    dsend,
    dret,
    psend,
    precv,
    pdsend,
    pdrecv,
    xs,
    ss,
    act,
    dhid,
    gin,
    gout,
    acc,
    w_sem,
    line_sem,
    t_send,
    t_recv,
    send_sem,
    rx_sem,
    rs_sem,
    fsend_sem,
    fx_sem,
    fs_sem,
    bsend_sem,
    brecv_sem,
    dsend_sem,
    drecv_sem,
    psend_sem,
    precv_sem,
    pdsend_sem,
    pdrecv_sem,
):
    dp = lax.axis_index("dp")
    me = lax.axis_index("expert")
    other = 1 - dp
    loads = [
        pltpu.make_async_copy(source, target, w_sem.at[2 + n])
        for n, (source, target) in enumerate(
            ((routes_hbm, routes_ref), (gates_hbm, gates_ref), (x_hbm, x_ref), (g_hbm, g_ref))
        )
    ]
    for load in loads:
        load.start()

    barrier = pltpu.get_barrier_semaphore()

    def along(axis, step):
        z, y, x = me >> 4, (me >> 2) & 3, me & 3
        if axis == 0:
            z = (z + step) & 7
        elif axis == 1:
            y = (y + step) & 3
        else:
            x = (x + step) & 3
        return (dp, z * 16 + y * 4 + x)

    def greet(semaphore, axis):
        for step in (1, 7, 2, 6, 3, 5, 4) if axis == 0 else (1, 3, 2):
            pl.semaphore_signal(
                semaphore, inc=1, device_id=along(axis, step), device_id_type=MESH
            )

    for axis in range(3):
        greet(barrier, axis)
    pl.semaphore_signal(barrier, inc=1, device_id=(other, me), device_id_type=MESH)
    pl.semaphore_wait(barrier, 14)

    def hand(n, source, target):
        copies = []
        for side in range(2):
            copy = pltpu.make_async_remote_copy(
                source,
                target.at[side],
                t_send.at[n, side],
                t_recv.at[n, side],
                device_id=along(0, 1 - 2 * side),
                device_id_type=MESH,
            )
            copy.start()
            copies.append(copy)
        return copies

    hand_x = hand(1, x_hbm, near_x)
    load_in = pltpu.make_async_copy(win_hbm, win, w_sem.at[0])
    load_out = pltpu.make_async_copy(wout_hbm, wout, w_sem.at[1])
    load_in.start()
    load_out.start()
    greet(line_sem.at[0], 1)

    row, col = iota((ROWS, ROWS), 0), iota((ROWS, ROWS), 1)
    number_of_row, number_of_col = (row & 31) * 4 + (row >> 5), (col & 31) * 4 + (col >> 5)
    reorder = (row == number_of_col).astype(F32).astype(BF16)
    earlier = (number_of_row < number_of_col).astype(F32).astype(BF16)
    raw_table[...] = jnp.zeros_like(raw_table)
    loads[0].wait()
    loads[1].wait()
    raw_table[0:2, :] = routes_ref[...].astype(F32)
    raw_table[2:4, :] = gates_ref[...].astype(F32)
    table[...] = dot(raw_table[...].astype(BF16), reorder)
    hand_table = hand(0, table, near_table)

    def stack(source, target):
        for h in range(HEADS):
            for part in range(4):
                at = h * WIDTH + part * 256
                target[pl.ds(part * ROWS + h * TOK, TOK), :] = source[:, at : at + 256]

    pl.semaphore_wait(line_sem.at[0], 3)
    greet(line_sem.at[1], 2)

    def chosen(source, lines, first_line, origin, base):
        shape = (lines, ROWS)
        line = iota(shape, 0) + first_line
        expert = partner(origin, base + (line >> 4), 1).astype(F32)
        first, second = expert == source[0:1], expert == source[1:2]
        member = jnp.where(first | second, 1.0, 0.0)
        count = dot(member.astype(BF16), earlier)
        hit = jnp.where(count == (line & 3).astype(F32), member, 0.0)
        return line, first, hit

    def plan(unit, source, lines, first_line, origin, base):
        line, first, hit = chosen(source, lines, first_line, origin, base)
        gated = hit * jnp.where(first, source[2:3], source[3:4])
        part = (line >> 2) & 3
        at = pl.ds(first_line, lines)
        for p in range(4):
            cols = slice(p * ROWS, p * ROWS + ROWS)
            plan_x[unit, at, cols] = jnp.where(part == p, hit, 0.0).astype(BF16)
            plan_s[unit, at, cols] = jnp.where(part == p, gated, 0.0).astype(BF16)

    def build(unit, side, plans, stacks, sends):
        start, stop = (side * 8, side * 8 + 8) if unit == HALVES else (0, 16)
        tokens = stacks if side is None else stacks.at[side]
        made = dot(plans[unit, start * 16 : stop * 16, :], tokens[...]).astype(BF16)
        sends[unit * 16 + start : unit * 16 + stop] = made.reshape(stop - start, 16, 256)

    def post(units, sends, recvs, sems):
        for unit, side in units:
            if unit in (0, 1, OWN):
                k = unit * 16
                pltpu.make_async_copy(sends.at[k], recvs.at[k], sems.at[unit // 2]).start()

        def push(i, carry):
            for unit, side in units:
                if unit in (0, 1, OWN):
                    place = lax.rem(i - 1 + 4 * unit, 15) + 1
                else:
                    place = (i + 5 * unit) & 15
                k = unit * 16 + place
                lift = 0 if side is None else 2 * side - 1
                if unit == HALVES:
                    lift = 2 * (place >> 3) - 1
                copy = pltpu.make_async_remote_copy(
                    sends.at[k],
                    recvs.at[k],
                    send_sem,
                    sems.at[unit // 2],
                    device_id=(dp, partner(me, k, 1, lift)),
                    device_id_type=MESH,
                )
                if unit in (0, 1, OWN):
                    pl.when(i > 0)(copy.start)
                else:
                    copy.start()
            return carry

        lax.fori_loop(0, 16, push, 0)

    plan(OWN, table[...], 256, 0, me, OWN * 16)
    loads[2].wait()
    loads[3].wait()
    stack(x_ref, stack_x)
    stack(g_ref, stack_g)
    pl.semaphore_wait(line_sem.at[1], 3)
    for plans, stacks, sends, recvs, sems in (
        (plan_x, stack_x, send_x, recv_x, rx_sem),
        (plan_s, stack_g, send_s, recv_s, rs_sem),
    ):
        build(OWN, None, plans, stacks, sends)
        post(((OWN, None),), sends, recvs, sems)
    hand_g = hand(2, g_hbm, near_g)
    for side in range(2):
        hand_table[side].wait_recv()
    origins = (along(0, -1)[1], along(0, 1)[1])
    units = ((2, 0), (3, 1), (0, 0), (1, 1), (6, 0), (7, 1), (HALVES, 0), (HALVES, 1))
    for unit, side in units:
        lines, first_line = (128, 128 * side) if unit == HALVES else (256, 0)
        plan(unit, near_table[side], lines, first_line, origins[side], unit * 16)
    gin[...] = jnp.zeros_like(gin)
    gout[...] = jnp.zeros_like(gout)
    acc[...] = jnp.zeros_like(acc)
    kinds = (
        (hand_x, near_x, near_stack_x, plan_x, send_x, recv_x, rx_sem),
        (hand_g, near_g, near_stack_g, plan_s, send_s, recv_s, rs_sem),
    )

    def arrive(kind):
        handed, raw, stacks = kinds[kind][:3]
        for side in range(2):
            handed[side].wait_recv()
            stack(raw.at[side], stacks.at[side])

    def relay(kind, some):
        stacks, plans, sends, recvs, sems = kinds[kind][2:]
        for unit, side in some:
            build(unit, side, plans, stacks, sends)
        post(tuple(pair for pair in some if pair != (HALVES, 1)), sends, recvs, sems)

    arrive(0)
    relay(0, units[:4])
    arrive(1)
    relay(1, units[:4])
    relay(0, units[4:])
    relay(1, units[4:])
    load_in.wait()
    load_out.wait()

    size = GROUP * 16
    to, frm = iota((size, size), 0), iota((size, size), 1)
    unpack = (
        (frm == ((to & 63) >> 2) * 16 + (to >> 6) * 4 + (to & 3)).astype(F32).astype(BF16)
    )
    pack = (to == ((frm & 63) >> 2) * 16 + (frm >> 6) * 4 + (frm & 3)).astype(F32).astype(BF16)

    def open_rows(source, target, j, base):
        for b in range(CH // GROUP):
            raw = source[pl.ds(j * CH + b * GROUP, GROUP)].reshape(size, 256)
            rows = dot(unpack, raw).astype(BF16)
            at = base + b * 64
            for p in range(4):
                target[at : at + 64, p * 256 : p * 256 + 256] = rows[p * 64 : p * 64 + 64]

    def step(j, carry):
        mine = pl.ds(j * CH, CH)
        forwards = []
        for n, (got, passed, sem, fsem) in enumerate(
            ((recv_x, recv2_x, rx_sem, fx_sem), (recv_s, recv2_s, rs_sem, fs_sem))
        ):
            pltpu.make_async_copy(got.at[mine], got.at[mine], sem.at[j]).wait()
            forward = pltpu.make_async_remote_copy(
                got.at[mine],
                passed.at[mine],
                fsend_sem.at[n, j],
                fsem.at[j],
                device_id=(other, me),
                device_id_type=MESH,
            )
            forward.start()
            forwards.append(forward)
            open_rows(got, (xs, ss)[n], j, 0)
        forwards[0].wait_recv()
        open_rows(recv2_x, xs, j, CROWS)
        forwards[1].wait_recv()
        open_rows(recv2_s, ss, j, CROWS)

        dots = jnp.zeros((2 * CROWS, 1), F32)
        for b in range(HID // 256):
            cols = slice(b * 256, b * 256 + 256)
            hidden = dot(xs[...], win[:, cols])
            pulled = dot(ss[...], wout[cols, :], ((1,), (1,)))
            square = hidden * hidden
            tangent = jnp.tanh(0.7978845608028654 * (hidden + 0.044715 * square * hidden))
            active = (0.5 * hidden * (1.0 + tangent)).astype(BF16)
            slope = 0.5 * (1.0 + tangent) + 0.5 * hidden * (
                1.0 - tangent * tangent
            ) * 0.7978845608028654 * (1.0 + 3.0 * 0.044715 * square)
            act[:, cols] = active
            dhid[:, cols] = (pulled * slope).astype(BF16)
            dots = dots + jnp.sum(active.astype(F32) * pulled, axis=1, keepdims=True)
        partial = dot(dhid[...], win[...], ((1,), (1,)))
        psend[j] = partial[CROWS:].astype(BF16)
        wide = jnp.broadcast_to(dots, (2 * CROWS, 128))
        pdsend[j] = wide[CROWS:]
        swap = pltpu.make_async_remote_copy(
            psend.at[j],
            precv.at[j],
            psend_sem.at[j],
            precv_sem.at[j],
            device_id=(other, me),
            device_id_type=MESH,
        )
        swap_dots = pltpu.make_async_remote_copy(
            pdsend.at[j],
            pdrecv.at[j],
            pdsend_sem.at[j],
            pdrecv_sem.at[j],
            device_id=(other, me),
            device_id_type=MESH,
        )
        swap.start()
        swap_dots.start()
        for b in range(HID // 256):
            cols = slice(b * 256, b * 256 + 256)
            gout[cols, :] += dot(act[:, cols], ss[...], ((0,), (0,)))
            gin[cols, :] += dot(xs[:, cols], dhid[...], ((0,), (0,)))
        swap.wait_recv()
        swap_dots.wait_recv()
        whole = (partial[:CROWS] + precv[j].astype(F32)).astype(BF16)
        for b in range(CH // GROUP):
            rows = whole[b * 64 : b * 64 + 64]
            tall = jnp.concatenate([rows[:, p * 256 : p * 256 + 256] for p in range(4)], axis=0)
            back[pl.ds(j * CH + b * GROUP, GROUP)] = (
                dot(pack, tall).astype(BF16).reshape(GROUP, 16, 256)
            )
        all_dots = wide[:CROWS] + pdrecv[j]
        line, lane = iota((CROWS, 128), 0), iota((CROWS, 128), 1)
        spread = jnp.where((line & 3) == lane, all_dots, 0.0)
        gather = (iota((CH, CROWS), 0) == (iota((CH, CROWS), 1) >> 2)).astype(F32)
        dsend[mine] = dot(gather, spread, precision=lax.Precision.HIGHEST).reshape(CH, 1, 128)

        @pl.when(j == OWN // 2)
        def _():
            k = OWN * 16
            pltpu.make_async_copy(back.at[k], ret.at[k], brecv_sem.at[j]).start()
            pltpu.make_async_copy(dsend.at[k], dret.at[k], drecv_sem.at[j]).start()

        def push(i, c):
            k = j * CH + (i & 1) * 16 + (i >> 1)
            target = (dp, partner(me, k, -1))
            pltpu.make_async_remote_copy(
                back.at[k],
                ret.at[k],
                bsend_sem,
                brecv_sem.at[j],
                device_id=target,
                device_id_type=MESH,
            ).start()
            pltpu.make_async_remote_copy(
                dsend.at[k],
                dret.at[k],
                dsend_sem,
                drecv_sem.at[j],
                device_id=target,
                device_id_type=MESH,
            ).start()
            return c

        lax.fori_loop(jnp.where(j == OWN // 2, 1, 0), CH, push, 0)
        return carry

    lax.fori_loop(0, CHUNKS, step, 0)

    def remember(j, carry):
        _, _, hit = chosen(table[...], CH * 16, 0, me, j * CH)
        hits[j] = hit.T.astype(BF16)
        return carry

    lax.fori_loop(0, CHUNKS, remember, 0)
    gin_out[...] = gin[...].astype(BF16)
    gout_out[...] = gout[...].astype(BF16)

    expert = partner(me, iota((NE, ROWS), 0), 1).astype(F32)
    n0, n1 = raw_table[0:1], raw_table[1:2]
    first, second = expert == n0, expert == n1
    member = jnp.where(first | second, 1.0, 0.0)
    before = (row < col).astype(F32).astype(BF16)
    count = dot(member.astype(BF16), before)

    def collect(j, carry):
        mine = pl.ds(j * CH, CH)
        lane = iota((ROWS, CH * 16), 1)
        hit = hits[j].astype(F32)
        picks = jnp.concatenate(
            [jnp.where(((lane >> 2) & 3) == q, hit, 0.0).astype(BF16) for q in range(4)], axis=0
        )
        pltpu.make_async_copy(ret.at[mine], ret.at[mine], brecv_sem.at[j]).wait()
        acc[...] += dot(picks, ret[mine].reshape(CH * 16, 256))
        return carry

    lax.fori_loop(0, CHUNKS, collect, 0)
    for h in range(HEADS):
        for q in range(4):
            at = h * WIDTH + q * 256
            dx_out[:, at : at + 256] = acc[
                q * ROWS + h * TOK : q * ROWS + h * TOK + TOK, :
            ].astype(BF16)

    for j in range(CHUNKS):
        mine = pl.ds(j * CH, CH)
        pltpu.make_async_copy(dret.at[mine], dret.at[mine], drecv_sem.at[j]).wait()
    values = dret[...].reshape(NE, 128)
    picked = jnp.zeros((NE, ROWS), F32)
    for s in range(CAP):
        picked = picked + jnp.where(count == float(s), values[:, s : s + 1], 0.0)
    gate_out[0:1, :] = (
        jnp.sum(jnp.where(first, picked, 0.0), axis=0, keepdims=True) / raw_table[2:3]
    )
    gate_out[1:2, :] = (
        jnp.sum(jnp.where(second, picked, 0.0), axis=0, keepdims=True) / raw_table[3:4]
    )

    rest = pl.ds(1, NE - 1)
    for copy in hand_table + hand_x + hand_g:
        copy.wait_send()
    sent = pl.ds(3, NE - 3)
    pltpu.make_async_copy(send_x.at[sent], send_x.at[sent], send_sem).wait()
    pltpu.make_async_copy(send_s.at[sent], send_s.at[sent], send_sem).wait()
    pltpu.make_async_copy(back.at[rest], back.at[rest], bsend_sem).wait()
    pltpu.make_async_copy(dsend.at[rest], dsend.at[rest], dsend_sem).wait()
    for j in range(CHUNKS):
        mine = pl.ds(j * CH, CH)
        pltpu.make_async_copy(recv_x.at[mine], recv_x.at[mine], fsend_sem.at[0, j]).wait()
        pltpu.make_async_copy(recv_s.at[mine], recv_s.at[mine], fsend_sem.at[1, j]).wait()
        pltpu.make_async_copy(psend.at[j], psend.at[j], psend_sem.at[j]).wait()
        pltpu.make_async_copy(pdsend.at[j], pdsend.at[j], pdsend_sem.at[j]).wait()


def flush(dx, gate, gin, gout, dx_out, gate_out, gin_out, gout_out, sems):
    copies = [
        pltpu.make_async_copy(source, target, sems.at[n])
        for n, (source, target) in enumerate(
            ((gin, gin_out), (gout, gout_out), (dx, dx_out), (gate, gate_out))
        )
    ]
    for copy in copies:
        copy.start()
    for copy in copies:
        copy.wait()


def body(inputs, cotangent, gates, routes, w_in, w_out):
    vmem, hbm = pl.BlockSpec(memory_space=pltpu.VMEM), pl.BlockSpec(memory_space=pl.ANY)
    dma = pltpu.SemaphoreType.DMA
    shapes = (
        (inputs.shape, BF16),
        ((2, ROWS), F32),
        ((WIDTH, HID), BF16),
        ((HID, WIDTH), BF16),
    )
    outs = pl.pallas_call(
        kernel,
        out_shape=tuple(pltpu.VMEM(shape, kind) for shape, kind in shapes),
        in_specs=[hbm] * 6,
        out_specs=(vmem,) * 4,
        scratch_shapes=[
            pltpu.VMEM((WIDTH, HID), BF16),
            pltpu.VMEM((HID, WIDTH), BF16),
            pltpu.VMEM(routes.shape[::-1], jnp.int32),
            pltpu.VMEM(gates.shape[::-1], BF16),
            pltpu.VMEM(inputs.shape, BF16),
            pltpu.VMEM(inputs.shape, BF16),
            pltpu.VMEM((8, ROWS), F32),
            pltpu.VMEM((8, ROWS), F32),
            pltpu.VMEM((4 * ROWS, 256), BF16),
            pltpu.VMEM((4 * ROWS, 256), BF16),
            pltpu.VMEM((2, 8, ROWS), F32),
            pltpu.VMEM((2,) + inputs.shape, BF16),
            pltpu.VMEM((2,) + inputs.shape, BF16),
            pltpu.VMEM((2, 4 * ROWS, 256), BF16),
            pltpu.VMEM((2, 4 * ROWS, 256), BF16),
            pltpu.VMEM((CHUNKS, ROWS, CH * 16), BF16),
            pltpu.VMEM((8, 256, 4 * ROWS), BF16),
            pltpu.VMEM((8, 256, 4 * ROWS), BF16),
            pltpu.VMEM((NE, 16, 256), BF16),
            pltpu.VMEM((NE, 16, 256), BF16),
            pltpu.VMEM((NE, 16, 256), BF16),
            pltpu.VMEM((NE, 16, 256), BF16),
            pltpu.VMEM((NE, 16, 256), BF16),
            pltpu.VMEM((NE, 16, 256), BF16),
            pltpu.VMEM((NE, 16, 256), BF16),
            pltpu.VMEM((NE, 16, 256), BF16),
            pltpu.VMEM((NE, 1, 128), F32),
            pltpu.VMEM((NE, 1, 128), F32),
            pltpu.VMEM((CHUNKS, CROWS, WIDTH), BF16),
            pltpu.VMEM((CHUNKS, CROWS, WIDTH), BF16),
            pltpu.VMEM((CHUNKS, CROWS, 128), F32),
            pltpu.VMEM((CHUNKS, CROWS, 128), F32),
            pltpu.VMEM((2 * CROWS, WIDTH), BF16),
            pltpu.VMEM((2 * CROWS, WIDTH), BF16),
            pltpu.VMEM((2 * CROWS, HID), BF16),
            pltpu.VMEM((2 * CROWS, HID), BF16),
            pltpu.VMEM((WIDTH, HID), F32),
            pltpu.VMEM((HID, WIDTH), F32),
            pltpu.VMEM((4 * ROWS, 256), F32),
            dma((6,)),
            pltpu.SemaphoreType.REGULAR((2,)),
            dma((3, 2)),
            dma((3, 2)),
            dma,
            dma((CHUNKS,)),
            dma((CHUNKS,)),
            dma((2, CHUNKS)),
            dma((CHUNKS,)),
            dma((CHUNKS,)),
            dma,
            dma((CHUNKS,)),
            dma,
            dma((CHUNKS,)),
            dma((CHUNKS,)),
            dma((CHUNKS,)),
            dma((CHUNKS,)),
            dma((CHUNKS,)),
        ],
        compiler_params=pltpu.CompilerParams(
            collective_id=0, has_side_effects=True, vmem_limit_bytes=48 << 20
        ),
        name="experts",
    )(
        *(
            pltpu.with_memory_space_constraint(array, pltpu.HBM)
            for array in (routes.T, gates.T, inputs, cotangent, w_in[0], w_out[0])
        )
    )
    dx, gate, gin, gout = pl.pallas_call(
        flush,
        out_shape=tuple(jax.ShapeDtypeStruct(shape, kind) for shape, kind in shapes),
        in_specs=[vmem] * 4,
        out_specs=(hbm,) * 4,
        scratch_shapes=[dma((4,))],
        compiler_params=pltpu.CompilerParams(vmem_limit_bytes=1 << 20),
        name="flush",
    )(*outs)
    return dx, gate.T, gin[None], gout[None]


def solution(mesh):
    return jax.shard_map(
        body,
        mesh=mesh,
        in_specs=(
            P(("dp", "expert"), None),
            P(("dp", "expert"), None),
            P(("dp", "expert"), None),
            P(("dp", "expert"), None),
            P("expert", None, "dp"),
            P("expert", "dp", None),
        ),
        out_specs=(
            P(("dp", "expert"), None),
            P(("dp", "expert"), None),
            P("expert", None, "dp"),
            P("expert", "dp", None),
        ),
        check_vma=False,
    )
```

```python
import functools

import jax
import jax.numpy as jnp
from jax import lax
from jax.experimental import pallas as pl
from jax.experimental.pallas import tpu as pltpu
from jax.sharding import PartitionSpec as P

MESH = pl.DeviceIdType.MESH
F32 = jnp.float32
BF16 = jnp.bfloat16

HEADS = 4
WIDTH = 1024
HID = 1024
TOK = 32
ROWS = 128
NE = 128
CAP = 4
CHUNKS = 4
CH = NE // CHUNKS
GROUP = 16
CROWS = CH * CAP
OWN = 4
HALVES = 5


def offsets(k):
    high, low, place = k >> 6, (k >> 5) & 1, k & 15
    second, third, fourth = (1 - high) * low, high * (1 - low), high * low
    dz = (1 + 2 * second - 3 * third + fourth) * (1 - 2 * ((k >> 4) & 1)) + 2 * third
    return dz, place >> 2, place & 3


def partner(me, k, sign, lift=0):
    z, y, x = me >> 4, (me >> 2) & 3, me & 3
    dz, dy, dx = offsets(k)
    return (
        ((z + sign * dz + lift + 16) & 7) * 16
        + ((y + sign * dy + 4) & 3) * 4
        + ((x + sign * dx + 4) & 3)
    )


def iota(shape, axis):
    return lax.broadcasted_iota(jnp.int32, shape, axis)


def dot(a, b, contract=((1,), (0,)), precision=None):
    return lax.dot_general(
        a, b, (contract, ((), ())), precision=precision, preferred_element_type=F32
    )


def kernel(
    routes_hbm,
    gates_hbm,
    x_hbm,
    g_hbm,
    win_hbm,
    wout_hbm,
    dx_out,
    gate_out,
    gin_out,
    gout_out,
    win,
    wout,
    routes_ref,
    gates_ref,
    x_ref,
    g_ref,
    raw_table,
    table,
    stack_x,
    stack_g,
    near_table,
    near_x,
    near_g,
    near_stack_x,
    near_stack_g,
    hits,
    plan_x,
    plan_s,
    send_x,
    send_s,
    recv_x,
    recv_s,
    recv2_x,
    recv2_s,
    back,
    ret,
    dsend,
    dret,
    psend,
    precv,
    pdsend,
    pdrecv,
    xs,
    ss,
    act,
    dhid,
    gin,
    gout,
    acc,
    w_sem,
    line_sem,
    t_send,
    t_recv,
    send_sem,
    rx_sem,
    rs_sem,
    fsend_sem,
    fx_sem,
    fs_sem,
    bsend_sem,
    brecv_sem,
    dsend_sem,
    drecv_sem,
    psend_sem,
    precv_sem,
    pdsend_sem,
    pdrecv_sem,
):
    dp = lax.axis_index("dp")
    me = lax.axis_index("expert")
    other = 1 - dp
    loads = [
        pltpu.make_async_copy(source, target, w_sem.at[2 + n])
        for n, (source, target) in enumerate(
            ((routes_hbm, routes_ref), (gates_hbm, gates_ref), (x_hbm, x_ref), (g_hbm, g_ref))
        )
    ]
    for load in loads:
        load.start()

    barrier = pltpu.get_barrier_semaphore()

    def along(axis, step):
        z, y, x = me >> 4, (me >> 2) & 3, me & 3
        if axis == 0:
            z = (z + step) & 7
        elif axis == 1:
            y = (y + step) & 3
        else:
            x = (x + step) & 3
        return (dp, z * 16 + y * 4 + x)

    def greet(semaphore, axis):
        for step in (1, 7, 2, 6, 3, 5, 4) if axis == 0 else (1, 3, 2):
            pl.semaphore_signal(
                semaphore, inc=1, device_id=along(axis, step), device_id_type=MESH
            )

    for axis in range(3):
        greet(barrier, axis)
    pl.semaphore_signal(barrier, inc=1, device_id=(other, me), device_id_type=MESH)
    pl.semaphore_wait(barrier, 14)

    def hand(n, source, target):
        copies = []
        for side in range(2):
            copy = pltpu.make_async_remote_copy(
                source,
                target.at[side],
                t_send.at[n, side],
                t_recv.at[n, side],
                device_id=along(0, 1 - 2 * side),
                device_id_type=MESH,
            )
            copy.start()
            copies.append(copy)
        return copies

    hand_x = hand(1, x_hbm, near_x)
    load_in = pltpu.make_async_copy(win_hbm, win, w_sem.at[0])
    load_out = pltpu.make_async_copy(wout_hbm, wout, w_sem.at[1])
    load_in.start()
    load_out.start()
    greet(line_sem.at[0], 1)

    row, col = iota((ROWS, ROWS), 0), iota((ROWS, ROWS), 1)
    number_of_row, number_of_col = (row & 31) * 4 + (row >> 5), (col & 31) * 4 + (col >> 5)
    reorder = (row == number_of_col).astype(F32).astype(BF16)
    earlier = (number_of_row < number_of_col).astype(F32).astype(BF16)
    raw_table[...] = jnp.zeros_like(raw_table)
    loads[0].wait()
    loads[1].wait()
    raw_table[0:2, :] = routes_ref[...].astype(F32)
    raw_table[2:4, :] = gates_ref[...].astype(F32)
    table[...] = dot(raw_table[...].astype(BF16), reorder)
    hand_table = hand(0, table, near_table)

    def stack(source, target):
        for h in range(HEADS):
            for part in range(4):
                at = h * WIDTH + part * 256
                target[pl.ds(part * ROWS + h * TOK, TOK), :] = source[:, at : at + 256]

    pl.semaphore_wait(line_sem.at[0], 3)
    greet(line_sem.at[1], 2)

    def chosen(source, lines, first_line, origin, base):
        shape = (lines, ROWS)
        line = iota(shape, 0) + first_line
        expert = partner(origin, base + (line >> 4), 1).astype(F32)
        first, second = expert == source[0:1], expert == source[1:2]
        member = jnp.where(first | second, 1.0, 0.0)
        count = dot(member.astype(BF16), earlier)
        hit = jnp.where(count == (line & 3).astype(F32), member, 0.0)
        return line, first, hit

    def plan(unit, source, lines, first_line, origin, base):
        line, first, hit = chosen(source, lines, first_line, origin, base)
        gated = hit * jnp.where(first, source[2:3], source[3:4])
        part = (line >> 2) & 3
        at = pl.ds(first_line, lines)
        for p in range(4):
            cols = slice(p * ROWS, p * ROWS + ROWS)
            plan_x[unit, at, cols] = jnp.where(part == p, hit, 0.0).astype(BF16)
            plan_s[unit, at, cols] = jnp.where(part == p, gated, 0.0).astype(BF16)

    def build(unit, side, plans, stacks, sends):
        start, stop = (side * 8, side * 8 + 8) if unit == HALVES else (0, 16)
        tokens = stacks if side is None else stacks.at[side]
        made = dot(plans[unit, start * 16 : stop * 16, :], tokens[...]).astype(BF16)
        sends[unit * 16 + start : unit * 16 + stop] = made.reshape(stop - start, 16, 256)

    def post(units, sends, recvs, sems):
        for unit, side in units:
            if unit in (0, 1, OWN):
                k = unit * 16
                pltpu.make_async_copy(sends.at[k], recvs.at[k], sems.at[unit // 2]).start()

        def push(i, carry):
            for unit, side in units:
                if unit in (0, 1, OWN):
                    place = lax.rem(i + 14 + 4 * unit + 7 * dp, 15) + 1
                else:
                    place = (i + 5 * unit + 8 * dp) & 15
                k = unit * 16 + place
                lift = 0 if side is None else 2 * side - 1
                if unit == HALVES:
                    lift = 2 * (place >> 3) - 1
                copy = pltpu.make_async_remote_copy(
                    sends.at[k],
                    recvs.at[k],
                    send_sem,
                    sems.at[unit // 2],
                    device_id=(dp, partner(me, k, 1, lift)),
                    device_id_type=MESH,
                )
                if unit in (0, 1, OWN):
                    pl.when(i > 0)(copy.start)
                else:
                    copy.start()
            return carry

        lax.fori_loop(0, 16, push, 0)

    plan(OWN, table[...], 256, 0, me, OWN * 16)
    loads[2].wait()
    loads[3].wait()
    stack(x_ref, stack_x)
    stack(g_ref, stack_g)
    pl.semaphore_wait(line_sem.at[1], 3)
    for plans, stacks, sends, recvs, sems in (
        (plan_x, stack_x, send_x, recv_x, rx_sem),
        (plan_s, stack_g, send_s, recv_s, rs_sem),
    ):
        build(OWN, None, plans, stacks, sends)
        post(((OWN, None),), sends, recvs, sems)
    hand_g = hand(2, g_hbm, near_g)
    for side in range(2):
        hand_table[side].wait_recv()
    origins = (along(0, -1)[1], along(0, 1)[1])
    units = ((2, 0), (3, 1), (0, 0), (1, 1), (6, 0), (7, 1), (HALVES, 0), (HALVES, 1))
    for unit, side in units:
        lines, first_line = (128, 128 * side) if unit == HALVES else (256, 0)
        plan(unit, near_table[side], lines, first_line, origins[side], unit * 16)
    gin[...] = jnp.zeros_like(gin)
    gout[...] = jnp.zeros_like(gout)
    acc[...] = jnp.zeros_like(acc)
    kinds = (
        (hand_x, near_x, near_stack_x, plan_x, send_x, recv_x, rx_sem),
        (hand_g, near_g, near_stack_g, plan_s, send_s, recv_s, rs_sem),
    )

    def arrive(kind):
        handed, raw, stacks = kinds[kind][:3]
        for side in range(2):
            handed[side].wait_recv()
            stack(raw.at[side], stacks.at[side])

    def relay(kind, some):
        stacks, plans, sends, recvs, sems = kinds[kind][2:]
        for unit, side in some:
            build(unit, side, plans, stacks, sends)
        post(tuple(pair for pair in some if pair != (HALVES, 1)), sends, recvs, sems)

    arrive(0)
    relay(0, units[:4])
    arrive(1)
    relay(1, units[:4])
    relay(0, units[4:])
    relay(1, units[4:])
    load_in.wait()
    load_out.wait()

    size = GROUP * 16
    to, frm = iota((size, size), 0), iota((size, size), 1)
    unpack = (
        (frm == ((to & 63) >> 2) * 16 + (to >> 6) * 4 + (to & 3)).astype(F32).astype(BF16)
    )
    pack = (to == ((frm & 63) >> 2) * 16 + (frm >> 6) * 4 + (frm & 3)).astype(F32).astype(BF16)

    def open_rows(source, target, j, base):
        for b in range(CH // GROUP):
            raw = source[pl.ds(j * CH + b * GROUP, GROUP)].reshape(size, 256)
            rows = dot(unpack, raw).astype(BF16)
            at = base + b * 64
            for p in range(4):
                target[at : at + 64, p * 256 : p * 256 + 256] = rows[p * 64 : p * 64 + 64]

    def step(j, carry):
        mine = pl.ds(j * CH, CH)
        forwards = []
        for n, (got, passed, sem, fsem) in enumerate(
            ((recv_x, recv2_x, rx_sem, fx_sem), (recv_s, recv2_s, rs_sem, fs_sem))
        ):
            pltpu.make_async_copy(got.at[mine], got.at[mine], sem.at[j]).wait()
            forward = pltpu.make_async_remote_copy(
                got.at[mine],
                passed.at[mine],
                fsend_sem.at[n, j],
                fsem.at[j],
                device_id=(other, me),
                device_id_type=MESH,
            )
            forward.start()
            forwards.append(forward)
            open_rows(got, (xs, ss)[n], j, 0)
        forwards[0].wait_recv()
        open_rows(recv2_x, xs, j, CROWS)
        forwards[1].wait_recv()
        open_rows(recv2_s, ss, j, CROWS)

        dots = jnp.zeros((2 * CROWS, 1), F32)
        for b in range(HID // 256):
            cols = slice(b * 256, b * 256 + 256)
            hidden = dot(xs[...], win[:, cols])
            pulled = dot(ss[...], wout[cols, :], ((1,), (1,)))
            square = hidden * hidden
            tangent = jnp.tanh(0.7978845608028654 * (hidden + 0.044715 * square * hidden))
            active = (0.5 * hidden * (1.0 + tangent)).astype(BF16)
            slope = 0.5 * (1.0 + tangent) + 0.5 * hidden * (
                1.0 - tangent * tangent
            ) * 0.7978845608028654 * (1.0 + 3.0 * 0.044715 * square)
            act[:, cols] = active
            dhid[:, cols] = (pulled * slope).astype(BF16)
            dots = dots + jnp.sum(active.astype(F32) * pulled, axis=1, keepdims=True)
        partial = dot(dhid[...], win[...], ((1,), (1,)))
        psend[j] = partial[CROWS:].astype(BF16)
        wide = jnp.broadcast_to(dots, (2 * CROWS, 128))
        pdsend[j] = wide[CROWS:]
        swap = pltpu.make_async_remote_copy(
            psend.at[j],
            precv.at[j],
            psend_sem.at[j],
            precv_sem.at[j],
            device_id=(other, me),
            device_id_type=MESH,
        )
        swap_dots = pltpu.make_async_remote_copy(
            pdsend.at[j],
            pdrecv.at[j],
            pdsend_sem.at[j],
            pdrecv_sem.at[j],
            device_id=(other, me),
            device_id_type=MESH,
        )
        swap.start()
        swap_dots.start()
        for b in range(HID // 256):
            cols = slice(b * 256, b * 256 + 256)
            gout[cols, :] += dot(act[:, cols], ss[...], ((0,), (0,)))
            gin[cols, :] += dot(xs[:, cols], dhid[...], ((0,), (0,)))
        swap.wait_recv()
        swap_dots.wait_recv()
        whole = (partial[:CROWS] + precv[j].astype(F32)).astype(BF16)
        for b in range(CH // GROUP):
            rows = whole[b * 64 : b * 64 + 64]
            tall = jnp.concatenate([rows[:, p * 256 : p * 256 + 256] for p in range(4)], axis=0)
            back[pl.ds(j * CH + b * GROUP, GROUP)] = (
                dot(pack, tall).astype(BF16).reshape(GROUP, 16, 256)
            )
        all_dots = wide[:CROWS] + pdrecv[j]
        line, lane = iota((CROWS, 128), 0), iota((CROWS, 128), 1)
        spread = jnp.where((line & 3) == lane, all_dots, 0.0)
        gather = (iota((CH, CROWS), 0) == (iota((CH, CROWS), 1) >> 2)).astype(F32)
        dsend[mine] = dot(gather, spread, precision=lax.Precision.HIGHEST).reshape(CH, 1, 128)

        @pl.when(j == OWN // 2)
        def _():
            k = OWN * 16
            pltpu.make_async_copy(back.at[k], ret.at[k], brecv_sem.at[j]).start()
            pltpu.make_async_copy(dsend.at[k], dret.at[k], drecv_sem.at[j]).start()

        def push(i, c):
            k = j * CH + (i & 1) * 16 + (((i >> 1) + 8 * dp) & 15)
            target = (dp, partner(me, k, -1))
            for source, place, left, came in (
                (back, ret, bsend_sem, brecv_sem),
                (dsend, dret, dsend_sem, drecv_sem),
            ):
                copy = pltpu.make_async_remote_copy(
                    source.at[k],
                    place.at[k],
                    left,
                    came.at[j],
                    device_id=target,
                    device_id_type=MESH,
                )
                pl.when(k != OWN * 16)(copy.start)
            return c

        lax.fori_loop(0, CH, push, 0)
        return carry

    lax.fori_loop(0, CHUNKS, step, 0)

    def remember(j, carry):
        _, _, hit = chosen(table[...], CH * 16, 0, me, j * CH)
        hits[j] = hit.T.astype(BF16)
        return carry

    lax.fori_loop(0, CHUNKS, remember, 0)
    gin_out[...] = gin[...].astype(BF16)
    gout_out[...] = gout[...].astype(BF16)

    expert = partner(me, iota((NE, ROWS), 0), 1).astype(F32)
    n0, n1 = raw_table[0:1], raw_table[1:2]
    first, second = expert == n0, expert == n1
    member = jnp.where(first | second, 1.0, 0.0)
    before = (row < col).astype(F32).astype(BF16)
    count = dot(member.astype(BF16), before)

    def collect(j, carry):
        mine = pl.ds(j * CH, CH)
        lane = iota((ROWS, CH * 16), 1)
        hit = hits[j].astype(F32)
        picks = jnp.concatenate(
            [jnp.where(((lane >> 2) & 3) == q, hit, 0.0).astype(BF16) for q in range(4)], axis=0
        )
        pltpu.make_async_copy(ret.at[mine], ret.at[mine], brecv_sem.at[j]).wait()
        acc[...] += dot(picks, ret[mine].reshape(CH * 16, 256))
        return carry

    lax.fori_loop(0, CHUNKS, collect, 0)
    for h in range(HEADS):
        for q in range(4):
            at = h * WIDTH + q * 256
            dx_out[:, at : at + 256] = acc[
                q * ROWS + h * TOK : q * ROWS + h * TOK + TOK, :
            ].astype(BF16)

    for j in range(CHUNKS):
        mine = pl.ds(j * CH, CH)
        pltpu.make_async_copy(dret.at[mine], dret.at[mine], drecv_sem.at[j]).wait()
    values = dret[...].reshape(NE, 128)
    picked = jnp.zeros((NE, ROWS), F32)
    for s in range(CAP):
        picked = picked + jnp.where(count == float(s), values[:, s : s + 1], 0.0)
    gate_out[0:1, :] = (
        jnp.sum(jnp.where(first, picked, 0.0), axis=0, keepdims=True) / raw_table[2:3]
    )
    gate_out[1:2, :] = (
        jnp.sum(jnp.where(second, picked, 0.0), axis=0, keepdims=True) / raw_table[3:4]
    )

    rest = pl.ds(1, NE - 1)
    for copy in hand_table + hand_x + hand_g:
        copy.wait_send()
    sent = pl.ds(3, NE - 3)
    pltpu.make_async_copy(send_x.at[sent], send_x.at[sent], send_sem).wait()
    pltpu.make_async_copy(send_s.at[sent], send_s.at[sent], send_sem).wait()
    pltpu.make_async_copy(back.at[rest], back.at[rest], bsend_sem).wait()
    pltpu.make_async_copy(dsend.at[rest], dsend.at[rest], dsend_sem).wait()
    for j in range(CHUNKS):
        mine = pl.ds(j * CH, CH)
        pltpu.make_async_copy(recv_x.at[mine], recv_x.at[mine], fsend_sem.at[0, j]).wait()
        pltpu.make_async_copy(recv_s.at[mine], recv_s.at[mine], fsend_sem.at[1, j]).wait()
        pltpu.make_async_copy(psend.at[j], psend.at[j], psend_sem.at[j]).wait()
        pltpu.make_async_copy(pdsend.at[j], pdsend.at[j], pdsend_sem.at[j]).wait()


def flush(dx, gate, gin, gout, dx_out, gate_out, gin_out, gout_out, sems):
    copies = [
        pltpu.make_async_copy(source, target, sems.at[n])
        for n, (source, target) in enumerate(
            ((gin, gin_out), (gout, gout_out), (dx, dx_out), (gate, gate_out))
        )
    ]
    for copy in copies:
        copy.start()
    for copy in copies:
        copy.wait()


def body(inputs, cotangent, gates, routes, w_in, w_out):
    vmem, hbm = pl.BlockSpec(memory_space=pltpu.VMEM), pl.BlockSpec(memory_space=pl.ANY)
    dma = pltpu.SemaphoreType.DMA
    shapes = (
        (inputs.shape, BF16),
        ((2, ROWS), F32),
        ((WIDTH, HID), BF16),
        ((HID, WIDTH), BF16),
    )
    outs = pl.pallas_call(
        kernel,
        out_shape=tuple(pltpu.VMEM(shape, kind) for shape, kind in shapes),
        in_specs=[hbm] * 6,
        out_specs=(vmem,) * 4,
        scratch_shapes=[
            pltpu.VMEM((WIDTH, HID), BF16),
            pltpu.VMEM((HID, WIDTH), BF16),
            pltpu.VMEM(routes.shape[::-1], jnp.int32),
            pltpu.VMEM(gates.shape[::-1], BF16),
            pltpu.VMEM(inputs.shape, BF16),
            pltpu.VMEM(inputs.shape, BF16),
            pltpu.VMEM((8, ROWS), F32),
            pltpu.VMEM((8, ROWS), F32),
            pltpu.VMEM((4 * ROWS, 256), BF16),
            pltpu.VMEM((4 * ROWS, 256), BF16),
            pltpu.VMEM((2, 8, ROWS), F32),
            pltpu.VMEM((2,) + inputs.shape, BF16),
            pltpu.VMEM((2,) + inputs.shape, BF16),
            pltpu.VMEM((2, 4 * ROWS, 256), BF16),
            pltpu.VMEM((2, 4 * ROWS, 256), BF16),
            pltpu.VMEM((CHUNKS, ROWS, CH * 16), BF16),
            pltpu.VMEM((8, 256, 4 * ROWS), BF16),
            pltpu.VMEM((8, 256, 4 * ROWS), BF16),
            pltpu.VMEM((NE, 16, 256), BF16),
            pltpu.VMEM((NE, 16, 256), BF16),
            pltpu.VMEM((NE, 16, 256), BF16),
            pltpu.VMEM((NE, 16, 256), BF16),
            pltpu.VMEM((NE, 16, 256), BF16),
            pltpu.VMEM((NE, 16, 256), BF16),
            pltpu.VMEM((NE, 16, 256), BF16),
            pltpu.VMEM((NE, 16, 256), BF16),
            pltpu.VMEM((NE, 1, 128), F32),
            pltpu.VMEM((NE, 1, 128), F32),
            pltpu.VMEM((CHUNKS, CROWS, WIDTH), BF16),
            pltpu.VMEM((CHUNKS, CROWS, WIDTH), BF16),
            pltpu.VMEM((CHUNKS, CROWS, 128), F32),
            pltpu.VMEM((CHUNKS, CROWS, 128), F32),
            pltpu.VMEM((2 * CROWS, WIDTH), BF16),
            pltpu.VMEM((2 * CROWS, WIDTH), BF16),
            pltpu.VMEM((2 * CROWS, HID), BF16),
            pltpu.VMEM((2 * CROWS, HID), BF16),
            pltpu.VMEM((WIDTH, HID), F32),
            pltpu.VMEM((HID, WIDTH), F32),
            pltpu.VMEM((4 * ROWS, 256), F32),
            dma((6,)),
            pltpu.SemaphoreType.REGULAR((2,)),
            dma((3, 2)),
            dma((3, 2)),
            dma,
            dma((CHUNKS,)),
            dma((CHUNKS,)),
            dma((2, CHUNKS)),
            dma((CHUNKS,)),
            dma((CHUNKS,)),
            dma,
            dma((CHUNKS,)),
            dma,
            dma((CHUNKS,)),
            dma((CHUNKS,)),
            dma((CHUNKS,)),
            dma((CHUNKS,)),
            dma((CHUNKS,)),
        ],
        compiler_params=pltpu.CompilerParams(
            collective_id=0, has_side_effects=True, vmem_limit_bytes=48 << 20
        ),
        name="experts",
    )(
        *(
            pltpu.with_memory_space_constraint(array, pltpu.HBM)
            for array in (routes.T, gates.T, inputs, cotangent, w_in[0], w_out[0])
        )
    )
    dx, gate, gin, gout = pl.pallas_call(
        flush,
        out_shape=tuple(jax.ShapeDtypeStruct(shape, kind) for shape, kind in shapes),
        in_specs=[vmem] * 4,
        out_specs=(hbm,) * 4,
        scratch_shapes=[dma((4,))],
        compiler_params=pltpu.CompilerParams(vmem_limit_bytes=1 << 20),
        name="flush",
    )(*outs)
    return dx, gate.T, gin[None], gout[None]


def solution(mesh):
    return jax.shard_map(
        body,
        mesh=mesh,
        in_specs=(
            P(("dp", "expert"), None),
            P(("dp", "expert"), None),
            P(("dp", "expert"), None),
            P(("dp", "expert"), None),
            P("expert", None, "dp"),
            P("expert", "dp", None),
        ),
        out_specs=(
            P(("dp", "expert"), None),
            P(("dp", "expert"), None),
            P("expert", None, "dp"),
            P("expert", "dp", None),
        ),
        check_vma=False,
    )
```
